1024 devices in a mesh: enc: 64 (over y, x, core), pb: 16 (over z).
Axes of the slice: x: 4, y: 8, z: 16, core: 2. Of those that a mesh axis runs over, the one named last changes fastest.
Arguments:
- queries: bfloat16 [64, 3072, 4096], P('enc', 'pb'), as said below
- passages: bfloat16 [64, 128, 4096], P('enc', 'pb'), as said below
- table: bfloat16 [16, 2048, 2, 4096], P('pb', 'enc'), may hold values from -0.09375 to 0.09375
- neg_blocks: int32 [64, 3072, 16], P('enc', 'pb'), may hold values from 0 to 2047, as said below
- block_lists: int32 [64, 16, 64, 1], P('enc', 'pb'), may hold values from 0 to 31, as said below
- block_counts: int32 [64, 16, 64], P('enc', 'pb'), may hold values from 0 to 1, as said below
- pos_index: int32 [64, 3072], P('enc', 'pb'), may hold values from 0 to 127
Outputs:
- losses: float32 [64, 3072], P('enc', 'pb')
- passage_grads: float32 [64, 128, 4096], P('enc', 'pb')
- table_grads: float32 [16, 2048, 2, 4096], P('pb', 'enc')
The draws below stay inside these ranges and needn't reach their ends.
Inputs may be any that keep to these rules, and one draw needn't show every extreme that they name: `queries`: entries lie within the stated range. `passages`: entries lie within the stated range. `neg_blocks`: the 16 ids of a query name blocks of 16 different owners (owner = id // 32); for owner o the id is o * 32 + block_lists[e, p, o, c] for some c < block_counts[e, p, o] of the query's device. `block_lists`: the 1 entries of one device and one owner are different blocks. `block_counts`: each count is 0 or 1; for every device all but 64 // 4 owners have 1.
All inputs are finite; a program needn't handle non-finite values.
Results may differ from the reference program's by a relative error of at most 0.015.
Values may be sent and summed in bfloat16 or wider, within the bound.
A program may use at most 32 MiB of HBM per device.

```python
import jax
import jax.numpy as jnp
from jax import lax

D = 4096
Q_DEV = 192
BLK_DEV = 32
BR = 2
CAP = 1
NB = 16
QG = 3072
NP = 128
BLOCKS = 2048
N_ENC = 64
N_PB = 16


def embed_pair(key, mixing):
    key = jax.random.fold_in(key, 11)
    keys = jax.random.split(key, 2)
    pass_shape = (N_ENC, NP, D)
    query_shape = (N_ENC, QG, D)
    normal_pass = jnp.clip(jax.random.normal(keys[0], pass_shape, jnp.float32), -4.0, 4.0) / 64.0
    normal_query = jnp.clip(jax.random.normal(keys[1], query_shape, jnp.float32), -4.0, 4.0) / 64.0
    passage_rows = normal_pass
    query_rows = normal_query
    pass_ids = jnp.arange(NP, dtype=jnp.int32)[None, :, None]
    next_row = (pass_ids % 8 == 1).astype(jnp.float32) * mixing
    passage_rows = passage_rows * (1.0 - next_row)
    query_ids = jnp.arange(QG, dtype=jnp.int32)
    row_ids = query_ids[None, :, None]
    lead_row = (row_ids % 8 == 0).astype(jnp.float32) * mixing
    query_rows = query_rows * (1.0 - lead_row)
    return (query_rows, passage_rows)


def block_plan(key):
    key = jax.random.fold_in(key, 23)
    keys = jax.random.split(key, 7)
    owner_ids = jnp.arange(N_ENC, dtype=jnp.int32)
    order_key = jax.random.randint(keys[0], (N_ENC, N_PB, N_ENC), 0, 1 << 20) * N_ENC + owner_ids
    ranking = jnp.argsort(jnp.argsort(order_key, axis=-1), axis=-1).astype(jnp.int32)
    active = ranking < N_ENC - N_ENC // 4
    counts = jnp.where(active, CAP, 0).astype(jnp.int32)
    offset = jax.random.randint(keys[1], (1, N_PB, N_ENC, 1), 0, BLK_DEV)
    first_pick = jax.random.randint(keys[2], (N_ENC, N_PB, N_ENC, 1), 0, BLK_DEV)
    second_pick = jax.random.randint(keys[3], (N_ENC, N_PB, N_ENC, 1), 0, BLK_DEV)
    third_pick = jax.random.randint(keys[4], (N_ENC, N_PB, N_ENC, 1), 0, BLK_DEV)
    hot_pick = jnp.minimum(jnp.minimum(first_pick, second_pick), third_pick)
    lists = ((offset + hot_pick + jnp.arange(CAP, dtype=jnp.int32)) % BLK_DEV).astype(jnp.int32)
    pick_key = jax.random.randint(keys[5], (N_ENC, N_PB, Q_DEV, N_ENC), 0, 1 << 20) * N_ENC + owner_ids
    pick_key = pick_key + jnp.where(active[:, :, None, :], 0, 1 << 29)
    chosen = jnp.argsort(pick_key, axis=-1)[..., :NB].astype(jnp.int32)
    slot_pick = jax.random.randint(keys[6], (N_ENC, N_PB, Q_DEV, NB), 0, CAP)
    flat_lists = jnp.broadcast_to(lists.reshape(N_ENC, N_PB, 1, N_ENC * CAP), (N_ENC, N_PB, Q_DEV, N_ENC * CAP))
    listed = jnp.take_along_axis(flat_lists, chosen * CAP + slot_pick, axis=-1)
    negatives = (chosen * BLK_DEV + listed).reshape(N_ENC, QG, NB).astype(jnp.int32)
    return (negatives, lists, counts)


def draw_queries(key, part):
    query_rows, passage_rows = embed_pair(key, 0.0)
    return query_rows.astype(jnp.bfloat16)


def draw_passages(key, part):
    query_rows, passage_rows = embed_pair(key, 0.0)
    return passage_rows.astype(jnp.bfloat16)


def draw_neg_blocks(key, part):
    negatives, lists, counts = block_plan(key)
    return negatives


def draw_block_lists(key, part):
    negatives, lists, counts = block_plan(key)
    return lists


def draw_block_counts(key, part):
    negatives, lists, counts = block_plan(key)
    return counts


def plant(result, own_key, least, high):
    shape = result.shape
    index_at = [jax.random.randint(jax.random.fold_in(own_key, axis), (), 0, shape[axis]) for axis in range(len(shape))]
    result = result.at[tuple(index_at)].set(least)
    longest = shape.index(max(shape))
    index_at[longest] = (index_at[longest] + 1) % shape[longest]
    return result.at[tuple(index_at)].set(high)


def block_levels(stream_key, extent, cuts, low, top_value):
    def one(dim, parts):
        heights = jax.random.uniform(jax.random.fold_in(jax.random.fold_in(stream_key, 6), dim), (parts,), jnp.float32, low / len(cuts), top_value / len(cuts))
        return jnp.repeat(jnp.exp(heights), extent[dim] // parts).reshape((-1,) + (1,) * (len(extent) - dim - 1))

    factor_of = one(*cuts[0])
    for cut in cuts[1:]:
        factor_of = factor_of * one(*cut)
    return factor_of


def bell_draw(stream_key, dims, spread, reach, pieces=(), held_as=jnp.bfloat16):
    array = jax.random.normal(stream_key, dims, jnp.float32) * spread
    if len(pieces) > 0:
        array = block_levels(stream_key, dims, pieces, -0.22, 0.18) * array
    return jnp.clip(array, min=-reach, max=reach).astype(held_as)


def setup_inputs(seed: int = 0) -> dict:
    key_of = jax.random.split(jax.random.key(seed), 8)
    return {
        "queries": draw_queries(jax.random.fold_in(key_of[7], 71), 0),
        "passages": draw_passages(jax.random.fold_in(key_of[7], 71), 0),
        "table": bell_draw(key_of[2], (N_PB, BLOCKS, BR, D), D ** -0.5, 0.09375, ((0, 16), (1, 64))),
        "neg_blocks": draw_neg_blocks(jax.random.fold_in(key_of[7], 71), 0),
        "block_lists": draw_block_lists(jax.random.fold_in(key_of[7], 71), 0),
        "block_counts": draw_block_counts(jax.random.fold_in(key_of[7], 71), 0),
        "pos_index": plant(jax.random.randint(key_of[6], (N_ENC, QG), 0, NP), jax.random.fold_in(key_of[6], 1), 0, NP - 1).astype(jnp.int32),
    }


score_scale = 50.0


def group_terms(query_group, passage_group, table, neg_group, list_group, count_group, label_group):
    in_logits = jnp.dot(query_group, passage_group.T, preferred_element_type=jnp.float32) * score_scale
    owner_ids = jnp.arange(N_ENC, dtype=jnp.int32)
    shard_ids = jnp.arange(N_PB, dtype=jnp.int32)
    block_ids = owner_ids[None, :, None] * BLK_DEV + list_group
    fetched = table[shard_ids[:, None, None], block_ids]
    hard_rows = fetched.reshape(N_PB, N_ENC * CAP * BR, D)
    query_blocks = query_group.reshape(N_PB, Q_DEV, D)
    hard_logits = jnp.einsum("pqd,prd->pqr", query_blocks.astype(jnp.float32), hard_rows.astype(jnp.float32), precision=lax.Precision.HIGHEST) * score_scale
    hard_logits = hard_logits.reshape(QG, N_ENC * CAP * BR)
    named_owner = jnp.any((neg_group // BLK_DEV)[:, :, None] == owner_ids[None, None, :], axis=1)
    named_owner = named_owner.reshape(N_PB, Q_DEV, N_ENC)
    usable_slot = jnp.arange(CAP, dtype=jnp.int32)[None, None, :] < count_group[:, :, None]
    live_mask = named_owner[:, :, :, None, None] & usable_slot[:, None, :, :, None]
    live_mask = jnp.broadcast_to(live_mask, (N_PB, Q_DEV, N_ENC, CAP, BR)).reshape(QG, N_ENC * CAP * BR)
    row_max = jnp.maximum(jnp.max(in_logits, axis=1), jnp.max(jnp.where(live_mask, hard_logits, -jnp.inf), axis=1))
    row_total = jnp.sum(jnp.exp(in_logits - row_max[:, None]), axis=1)
    row_total = row_total + jnp.sum(jnp.where(live_mask, jnp.exp(hard_logits - row_max[:, None]), 0.0), axis=1)
    row_lse = row_max + jnp.log(row_total)
    picked = jnp.take_along_axis(in_logits, label_group[:, None], axis=1)[:, 0]
    losses = row_lse - picked
    target = (jnp.arange(NP, dtype=jnp.int32)[None, :] == label_group[:, None]).astype(jnp.float32)
    in_weights = ((jnp.exp(in_logits - row_lse[:, None]) - target) * score_scale).astype(jnp.bfloat16)
    hard_weights = (jnp.where(live_mask, jnp.exp(hard_logits - row_lse[:, None]), 0.0) * score_scale).astype(jnp.bfloat16)
    passage_grads = jnp.dot(in_weights.T, query_group, preferred_element_type=jnp.float32)
    block_terms = jnp.einsum("pqr,pqd->prd", hard_weights.reshape(N_PB, Q_DEV, N_ENC * CAP * BR).astype(jnp.float32), query_blocks.astype(jnp.float32), precision=lax.Precision.HIGHEST)
    return losses, passage_grads, block_terms.reshape(N_PB, N_ENC, CAP, BR, D), block_ids


def reference(queries, passages, table, neg_blocks, block_lists, block_counts, pos_index):
    shard_ids = jnp.arange(N_PB, dtype=jnp.int32)

    def step_group(carried, inputs):
        query_group, passage_group, neg_group, list_group, count_group, label_group = inputs
        losses, passage_grads, block_terms, block_ids = group_terms(query_group, passage_group, table, neg_group, list_group, count_group, label_group)
        carried = carried.at[shard_ids[:, None, None], block_ids].add(block_terms)
        return carried, (losses, passage_grads)

    start_grads = jnp.zeros((N_PB, BLOCKS, BR, D), jnp.float32)
    table_grads, stacked = lax.scan(step_group, start_grads, (queries, passages, neg_blocks, block_lists, block_counts, pos_index))
    return stacked[0], stacked[1], table_grads
```

```python
import functools

import jax
import jax.numpy as jnp
from jax import lax
from jax.experimental import pallas as pl
from jax.experimental.pallas import tpu as pltpu
from jax.sharding import PartitionSpec as P

score_scale = 50.0
lanes = 128
chips_x = 4
cores = 2
f32 = jnp.float32
bf16 = jnp.bfloat16


def partner(me, step, count):
    per_row = chips_x * cores
    rows = count // per_row
    y = lax.rem(me // per_row + step // per_row, rows)
    x = lax.rem((me // cores) % chips_x + (step // cores) % chips_x, chips_x)
    core = lax.rem(me % cores + step % cores, cores)
    return (y * chips_x + x) * cores + core


def exchange_kernel(
    n,
    m,
    q_hbm,
    p_ref,
    table_hbm,
    neg_ref,
    lists_ref,
    counts_ref,
    pos_ref,
    losses_ref,
    pgrad_ref,
    terms_ref,
    ids_ref,
    q_v,
    table_v,
    id_send,
    id_recv,
    id_scalars,
    fsend,
    fetched,
    wide,
    hard,
    pg,
    hard_w,
    in_w,
    pgp,
    tsend,
    rs_send,
    rs_recv,
    local_sem,
    id_sems,
    f_sems,
    t_sems,
    g_send,
    g_recv,
    r_send,
    r_recv,
):
    e = lax.axis_index("enc")
    z = lax.axis_index("pb")
    fwd = m // 2
    bwd = m - 1 - fwd
    up = lax.rem(z + 1, m)
    down = lax.rem(z + m - 1, m)
    pieces = fetched.shape[1]
    groups = pieces // 2
    width = q_v.shape[1]
    half = width // 2
    queries = q_v.shape[0]
    blocks = table_v.shape[0]

    barrier = pltpu.get_barrier_semaphore()

    def greet(s, carry):
        pl.semaphore_signal(barrier, inc=1, device_id={"enc": partner(e, s, n)})
        return carry

    lax.fori_loop(1, n, greet, 0)
    pl.semaphore_signal(barrier, inc=1, device_id={"pb": up})
    pl.semaphore_signal(barrier, inc=1, device_id={"pb": down})
    q_copy = pltpu.make_async_copy(q_hbm, q_v, local_sem.at[0])
    q_copy.start()
    table_copy = pltpu.make_async_copy(table_hbm, table_v, local_sem.at[1])
    table_copy.start()

    owner_row = lax.broadcasted_iota(jnp.int32, (n, n), 0)
    owner_col = lax.broadcasted_iota(jnp.int32, (n, n), 1)
    own_ids = jnp.sum(
        jnp.where(owner_row == owner_col, jnp.broadcast_to(lists_ref[...], (n, n)), 0),
        axis=1,
        keepdims=True,
    )
    id_send[...] = jnp.broadcast_to(own_ids, (n, lanes)).reshape(n, 1, lanes)
    own_rows = p_ref[...].astype(f32)
    pg[z] = jnp.concatenate([own_rows[:, :half], own_rows[:, half:]], axis=0).astype(bf16)

    pl.semaphore_wait(barrier, n + 1)

    def pass_on(side, t):
        origin = lax.rem(z + m - t, m) if side == 0 else lax.rem(z + t, m)
        return pltpu.make_async_remote_copy(
            src_ref=pg.at[origin],
            dst_ref=pg.at[origin],
            send_sem=g_send.at[side, t],
            recv_sem=g_recv.at[side, t],
            device_id={"pb": up if side == 0 else down},
        )

    def arrival(side, t):
        origin = lax.rem(z + m - t - 1, m) if side == 0 else lax.rem(z + t + 1, m)
        return pltpu.make_async_remote_copy(
            src_ref=pg.at[origin],
            dst_ref=pg.at[origin],
            send_sem=g_send.at[side, t],
            recv_sem=g_recv.at[side, t],
            device_id={"pb": up if side == 0 else down},
        )

    def ask(s, carry):
        peer = partner(e, s, n)
        pltpu.make_async_remote_copy(
            src_ref=id_send.at[peer],
            dst_ref=id_recv.at[e],
            send_sem=id_sems.at[0],
            recv_sem=id_sems.at[1],
            device_id={"enc": peer},
        ).start()
        return carry

    lax.fori_loop(1, n, ask, 0)
    pltpu.make_async_copy(id_send.at[e], id_recv.at[e], id_sems.at[1]).start()
    pass_on(0, 0).start()
    pass_on(1, 0).start()
    table_copy.wait()
    pltpu.make_async_copy(id_recv, id_recv, id_sems.at[1]).wait()
    scalar_copy = pltpu.make_async_copy(id_recv, id_scalars, local_sem.at[2])
    scalar_copy.start()
    scalar_copy.wait()

    def serve(s, carry):
        peer = partner(e, s, n)
        wanted = id_scalars[peer, 0, 0]
        ids_ref[peer] = wanted
        fsend[peer] = table_v[wanted]
        pltpu.make_async_remote_copy(
            src_ref=fsend.at[peer],
            dst_ref=fetched.at[e],
            send_sem=f_sems.at[0],
            recv_sem=f_sems.at[1],
            device_id={"enc": peer},
        ).start()
        return carry

    lax.fori_loop(1, n, serve, 0)
    own_wanted = id_scalars[e, 0, 0]
    ids_ref[e] = own_wanted
    fetched[e] = table_v[own_wanted]

    for t in range(fwd):
        arrival(0, t).wait_recv()
        if t + 1 < fwd:
            pass_on(0, t + 1).start()
        if t < bwd:
            arrival(1, t).wait_recv()
        if t + 1 < bwd:
            pass_on(1, t + 1).start()

    q_copy.wait()
    contract_last = (((1,), (1,)), ((), ()))
    all_rows = pg[...].reshape(m * 16, half)
    first = lax.dot_general(all_rows, q_v[:, :half], contract_last, preferred_element_type=f32)
    second = lax.dot_general(all_rows, q_v[:, half:], contract_last, preferred_element_type=f32)
    first = first.reshape(m, 2, 8, queries)[:, 0]
    second = second.reshape(m, 2, 8, queries)[:, 1]
    in_logits = ((first + second) * score_scale).reshape(m * 8, queries)

    owner_ids = lax.div(neg_ref[...], blocks)
    owner_list = lax.broadcasted_iota(jnp.int32, (n, queries), 0)
    named = jnp.zeros((n, queries), jnp.bool_)
    for k in range(neg_ref.shape[0]):
        named = named | (owner_list == jnp.broadcast_to(owner_ids[k : k + 1, :], (n, queries)))
    usable = jnp.sum(
        jnp.where(owner_row == owner_col, jnp.broadcast_to(counts_ref[...], (n, n)), 0),
        axis=1,
        keepdims=True,
    )
    live = jnp.where(named, jnp.broadcast_to(usable, (n, queries)), 0)
    live = jnp.concatenate([live, live], axis=0) > 0

    pltpu.make_async_copy(
        fetched.at[pl.ds(0, n - 1)], fetched.at[pl.ds(0, n - 1)], f_sems.at[1]
    ).wait()

    def widen(o, carry):
        wide[pl.ds(pl.multiple_of(o * pieces, pieces), pieces), :] = fetched[o].astype(f32)
        return carry

    lax.fori_loop(0, n, widen, 0, unroll=4)
    for j in range(groups):
        both = [wide[pl.ds(2 * j + r, n, pieces), :] for r in range(2)]
        hard[:, j * lanes : (j + 1) * lanes] = jnp.concatenate(both, axis=0).astype(bf16)
    hard_logits = (
        lax.dot_general(hard[...], q_v[...], contract_last, preferred_element_type=f32)
        * score_scale
    )

    top = jnp.maximum(
        jnp.max(in_logits, axis=0, keepdims=True),
        jnp.max(jnp.where(live, hard_logits, -jnp.inf), axis=0, keepdims=True),
    )
    total = jnp.sum(jnp.exp(in_logits - top), axis=0, keepdims=True) + jnp.sum(
        jnp.where(live, jnp.exp(hard_logits - top), 0.0), axis=0, keepdims=True
    )
    row_lse = top + jnp.log(total)
    hard_weights = jnp.where(live, jnp.exp(hard_logits - row_lse), 0.0) * score_scale
    hard_w[...] = hard_weights.astype(bf16)
    is_label = lax.broadcasted_iota(jnp.int32, in_logits.shape, 0) == pos_ref[...]
    picked = jnp.sum(jnp.where(is_label, in_logits, 0.0), axis=0, keepdims=True)
    losses_ref[...] = row_lse - picked
    in_weights = (jnp.exp(in_logits - row_lse) - jnp.where(is_label, 1.0, 0.0)) * score_scale
    in_w[...] = in_weights.astype(bf16)

    span = 4 * lanes
    for c in range(width // span):
        part = jnp.dot(
            hard_w[...], q_v[:, c * span : (c + 1) * span], preferred_element_type=f32
        )
        for k in range(4):
            for r in range(2):
                wide[pl.ds(2 * (4 * c + k) + r, n, pieces), :] = part[
                    r * n : (r + 1) * n, k * lanes : (k + 1) * lanes
                ]

    def give(s, carry):
        peer = partner(e, s, n)
        tsend[peer] = wide[pl.ds(pl.multiple_of(peer * pieces, pieces), pieces), :].astype(bf16)
        pltpu.make_async_remote_copy(
            src_ref=tsend.at[peer],
            dst_ref=terms_ref.at[e],
            send_sem=t_sems.at[0],
            recv_sem=t_sems.at[1],
            device_id={"enc": peer},
        ).start()
        return carry

    lax.fori_loop(1, n, give, 0)
    tsend[e] = wide[pl.ds(pl.multiple_of(e * pieces, pieces), pieces), :].astype(bf16)
    pltpu.make_async_copy(tsend.at[e], terms_ref.at[e], t_sems.at[1]).start()

    for c in range(width // span):
        part = jnp.dot(
            in_w[...], q_v[:, c * span : (c + 1) * span], preferred_element_type=f32
        )
        h, at = divmod(c * span, half)
        pgp[:, 8 * h : 8 * h + 8, at : at + span] = part.reshape(m, 8, span)

    def carry_on(side, t):
        return pltpu.make_async_remote_copy(
            src_ref=rs_send.at[side, t],
            dst_ref=rs_recv.at[side, t],
            send_sem=r_send.at[side, t],
            recv_sem=r_recv.at[side, t],
            device_id={"pb": up if side == 0 else down},
        )

    for t in range(fwd):
        for side in range(2):
            steps = bwd if side else fwd
            if t >= steps:
                continue
            target = lax.rem(z + m - (steps - t), m) if side else lax.rem(z + steps - t, m)
            held = pgp[target]
            if t > 0:
                carry_on(side, t - 1).wait_recv()
                held = held + rs_recv[side, t - 1].astype(f32)
            rs_send[side, t] = held.astype(bf16)
            carry_on(side, t).start()
    carry_on(0, fwd - 1).wait_recv()
    carry_on(1, bwd - 1).wait_recv()
    done = pgp[z] + rs_recv[0, fwd - 1].astype(f32) + rs_recv[1, bwd - 1].astype(f32)
    pgrad_ref[:, :half] = done[:8]
    pgrad_ref[:, half:] = done[8:]

    pltpu.make_async_copy(
        id_send.at[pl.ds(0, n - 1)], id_send.at[pl.ds(0, n - 1)], id_sems.at[0]
    ).wait()
    pltpu.make_async_copy(
        fsend.at[pl.ds(0, n - 1)], fsend.at[pl.ds(0, n - 1)], f_sems.at[0]
    ).wait()
    for side in range(2):
        for t in range(bwd if side else fwd):
            pass_on(side, t).wait_send()
            carry_on(side, t).wait_send()
    pltpu.make_async_copy(
        tsend.at[pl.ds(0, n - 1)], tsend.at[pl.ds(0, n - 1)], t_sems.at[0]
    ).wait()
    pltpu.make_async_copy(terms_ref, terms_ref, t_sems.at[1]).wait()


def collect_kernel(ids_ref, terms_ref, out_ref):
    out_ref[...] = jnp.zeros_like(out_ref)

    def add(s, carry):
        block = ids_ref[s]
        out_ref[block] += terms_ref[s].astype(f32)
        return carry

    lax.fori_loop(0, terms_ref.shape[0], add, 0)


def body(queries, passages, table, neg_blocks, block_lists, block_counts, pos_index):
    n = lax.axis_size("enc")
    m = lax.axis_size("pb")
    query_rows = queries[0]
    count, width = query_rows.shape
    blocks = table.shape[1]
    pieces = 2 * width // lanes
    table_rows = (
        table[0]
        .reshape(blocks, 2, width // lanes, lanes)
        .transpose(0, 2, 1, 3)
        .reshape(blocks, pieces, lanes)
    )
    whole = pl.BlockSpec(memory_space=pltpu.VMEM)
    anywhere = pl.BlockSpec(memory_space=pl.ANY)
    losses, passage_grads, terms, ids = pl.pallas_call(
        functools.partial(exchange_kernel, n, m),
        out_shape=(
            jax.ShapeDtypeStruct((1, count), f32),
            jax.ShapeDtypeStruct((8, width), f32),
            jax.ShapeDtypeStruct((n, pieces, lanes), bf16),
            jax.ShapeDtypeStruct((n,), jnp.int32),
        ),
        in_specs=[anywhere, whole, anywhere, whole, whole, whole, whole],
        out_specs=(whole, whole, anywhere, pl.BlockSpec(memory_space=pltpu.SMEM)),
        scratch_shapes=[
            pltpu.VMEM((count, width), bf16),
            pltpu.VMEM((blocks, pieces, lanes), bf16),
            pltpu.VMEM((n, 1, lanes), jnp.int32),
            pltpu.VMEM((n, 1, lanes), jnp.int32),
            pltpu.SMEM((n, 1, lanes), jnp.int32),
            pltpu.VMEM((n, pieces, lanes), bf16),
            pltpu.VMEM((n, pieces, lanes), bf16),
            pltpu.VMEM((n * pieces, lanes), f32),
            pltpu.VMEM((2 * n, width), bf16),
            pltpu.VMEM((m, 16, width // 2), bf16),
            pltpu.VMEM((2 * n, count), bf16),
            pltpu.VMEM((8 * m, count), bf16),
            pltpu.VMEM((m, 16, width // 2), f32),
            pltpu.VMEM((n, pieces, lanes), bf16),
            pltpu.VMEM((2, m // 2, 16, width // 2), bf16),
            pltpu.VMEM((2, m // 2, 16, width // 2), bf16),
            pltpu.SemaphoreType.DMA((3,)),
            pltpu.SemaphoreType.DMA((2,)),
            pltpu.SemaphoreType.DMA((2,)),
            pltpu.SemaphoreType.DMA((2,)),
            pltpu.SemaphoreType.DMA((2, m // 2)),
            pltpu.SemaphoreType.DMA((2, m // 2)),
            pltpu.SemaphoreType.DMA((2, m // 2)),
            pltpu.SemaphoreType.DMA((2, m // 2)),
        ],
        compiler_params=pltpu.CompilerParams(
            collective_id=0, has_side_effects=True, vmem_limit_bytes=40 << 20
        ),
        name="exchange",
    )(
        query_rows,
        passages[0],
        table_rows,
        neg_blocks[0].T,
        block_lists[0, 0].reshape(1, n),
        block_counts[0],
        pos_index,
    )
    table_grads = pl.pallas_call(
        collect_kernel,
        out_shape=jax.ShapeDtypeStruct((blocks, pieces, lanes), f32),
        in_specs=[pl.BlockSpec(memory_space=pltpu.SMEM), whole],
        out_specs=whole,
        compiler_params=pltpu.CompilerParams(vmem_limit_bytes=16 << 20),
        name="collect",
    )(ids, terms)
    table_grads = (
        table_grads.reshape(blocks, width // lanes, 2, lanes)
        .transpose(0, 2, 1, 3)
        .reshape(1, blocks, 2, width)
    )
    return (losses, passage_grads[None], table_grads)


def solution(mesh):
    in_specs = (
        P("enc", "pb", None),
        P("enc", "pb", None),
        P("pb", "enc", None, None),
        P("enc", "pb", None),
        P("enc", "pb", None, None),
        P("enc", "pb", None),
        P("enc", "pb"),
    )
    out_specs = (P("enc", "pb"), P("enc", "pb", None), P("pb", "enc", None, None))
    return jax.shard_map(body, mesh=mesh, in_specs=in_specs, out_specs=out_specs, check_vma=False)
```

```python
import functools

import jax
import jax.numpy as jnp
from jax import lax
from jax.experimental import pallas as pl
from jax.experimental.pallas import tpu as pltpu
from jax.sharding import PartitionSpec as P

score_scale = 50.0
lanes = 128
chips_x = 4
cores = 2
ring_cuts = 2
send_group = 16
collect_groups = 4
f32 = jnp.float32
bf16 = jnp.bfloat16


def zigzag(k, count):
    odd = k % 2
    return lax.rem(odd * ((k + 1) // 2) + (1 - odd) * (count - k // 2), count)


def partner(me, step, count):
    rows = count // (chips_x * cores)
    y = lax.rem(me // (chips_x * cores) + zigzag(step % rows, rows), rows)
    x = lax.rem((me // cores) % chips_x + zigzag((step // rows) % chips_x, chips_x), chips_x)
    core = lax.rem(me % cores + step // (rows * chips_x), cores)
    return (y * chips_x + x) * cores + core


def source(me, step, count):
    rows = count // (chips_x * cores)
    y = lax.rem(me // (chips_x * cores) + rows - zigzag(step % rows, rows), rows)
    x = lax.rem(
        (me // cores) % chips_x + chips_x - zigzag((step // rows) % chips_x, chips_x), chips_x
    )
    core = lax.rem(me % cores + step // (rows * chips_x), cores)
    return (y * chips_x + x) * cores + core


def exchange_kernel(
    n,
    m,
    q_hbm,
    p_hbm,
    table_hbm,
    neg_hbm,
    lists_hbm,
    counts_hbm,
    pos_hbm,
    losses_ref,
    pgrad_ref,
    terms_ref,
    ids_ref,
    q_v,
    p_ref,
    table_v,
    neg_ref,
    counts_ref,
    pos_ref,
    column_lists,
    all_lists,
    id_row,
    id_scalars,
    fsend,
    fetched,
    wide,
    hard,
    pg,
    hard_w,
    in_w,
    pgp,
    tsend,
    rs_send,
    rs_recv,
    local_sem,
    id_sems,
    f_sems,
    t_sems,
    g_send,
    g_recv,
    r_send,
    r_recv,
):
    e = lax.axis_index("enc")
    z = lax.axis_index("pb")
    fwd = m // 2
    bwd = m - 1 - fwd
    up = lax.rem(z + 1, m)
    down = lax.rem(z + m - 1, m)
    pieces = fetched.shape[1]
    groups = pieces // 2
    width = q_v.shape[1]
    cut_width = pg.shape[3]
    per_row = chips_x * cores
    rows = n // per_row
    row, place = e // per_row, e % per_row
    queries = q_v.shape[0]
    blocks = table_v.shape[0]

    barrier = pltpu.get_barrier_semaphore()

    def row_mate(k):
        return {"enc": row * per_row + lax.rem(place + k, per_row)}

    def column_mate(k):
        return {"enc": lax.rem(row + k, rows) * per_row + place}

    for k in range(1, per_row):
        pl.semaphore_signal(barrier, inc=1, device_id=row_mate(k))
    for k in range(1, rows):
        pl.semaphore_signal(barrier, inc=1, device_id=column_mate(k))
    pl.semaphore_signal(barrier, inc=1, device_id={"pb": up})
    pl.semaphore_signal(barrier, inc=1, device_id={"pb": down})
    loads = [
        pltpu.make_async_copy(source, place, local_sem.at[k])
        for k, (source, place) in enumerate(
            (
                (lists_hbm, column_lists.at[row]),
                (p_hbm, p_ref),
                (table_hbm, table_v),
                (counts_hbm, counts_ref),
                (neg_hbm, neg_ref),
                (pos_hbm, pos_ref),
                (q_hbm, q_v),
            )
        )
    ]
    for load in loads:
        load.start()

    owner_row = lax.broadcasted_iota(jnp.int32, (n, n), 0)
    owner_col = lax.broadcasted_iota(jnp.int32, (n, n), 1)
    loads[1].wait()
    own_rows = p_ref[...].astype(f32)
    for u in range(ring_cuts):
        at = 2 * u * cut_width
        halves = [own_rows[:, at + h * cut_width : at + (h + 1) * cut_width] for h in range(2)]
        pg[u, z] = jnp.concatenate(halves, axis=0).astype(bf16)
    loads[0].wait()

    pl.semaphore_wait(barrier, per_row + rows)

    def ring_copy(side, u, t, origin):
        return pltpu.make_async_remote_copy(
            src_ref=pg.at[u, origin],
            dst_ref=pg.at[u, origin],
            send_sem=g_send.at[side, u, t],
            recv_sem=g_recv.at[side, u, t],
            device_id={"pb": down if side else up},
        )

    def pass_on(side, u, t):
        return ring_copy(side, u, t, lax.rem(z + t if side else z + m - t, m))

    def arrival(side, u, t):
        return ring_copy(side, u, t, lax.rem(z + t + 1 if side else z + m - t - 1, m))

    def gather_step(t):
        for u in range(ring_cuts):
            for side, steps in ((0, fwd), (1, bwd)):
                if t < steps:
                    arrival(side, u, t).wait_recv()
                if t + 1 < steps:
                    pass_on(side, u, t + 1).start()

    def column_copy(k):
        return pltpu.make_async_remote_copy(
            src_ref=column_lists.at[row],
            dst_ref=column_lists.at[row],
            send_sem=id_sems.at[0],
            recv_sem=id_sems.at[1],
            device_id=column_mate(k),
        )

    def row_copy(k):
        return pltpu.make_async_remote_copy(
            src_ref=column_lists,
            dst_ref=all_lists.at[place],
            send_sem=id_sems.at[2],
            recv_sem=id_sems.at[3],
            device_id=row_mate(k),
        )

    def to_scalars(lists, slot):
        wanted = jnp.sum(
            jnp.where(owner_col[: lists.shape[0]] == e, lists, 0), axis=1, keepdims=True
        )
        id_row[slot] = jnp.sum(
            jnp.where(
                owner_row[: lists.shape[0]] == owner_col[: lists.shape[0]],
                jnp.broadcast_to(wanted, lists.shape),
                0,
            ),
            axis=0,
            keepdims=True,
        )
        copy = pltpu.make_async_copy(id_row.at[slot], id_scalars.at[slot], local_sem.at[7 + slot])
        copy.start()
        return copy

    def serve(slot, group, s, carry):
        peer = partner(e, s, n)
        asker = peer // per_row if slot == 0 else (peer % per_row) * rows + peer // per_row
        wanted = id_scalars[slot, 0, asker]
        ids_ref[peer] = wanted
        fsend[peer] = table_v[wanted]
        pltpu.make_async_remote_copy(
            src_ref=fsend.at[peer],
            dst_ref=fetched.at[e],
            send_sem=f_sems.at[0],
            recv_sem=f_sems.at[1 + group],
            device_id={"enc": peer},
        ).start()
        return carry

    for k in range(1, rows):
        column_copy(k).start()
    for u in range(ring_cuts):
        pass_on(0, u, 0).start()
        pass_on(1, u, 0).start()
    column_part = column_lists.at[pl.ds(0, rows - 1)]
    pltpu.make_async_copy(column_part, column_part, id_sems.at[1]).wait()
    for k in range(1, per_row):
        row_copy(k).start()
    early = to_scalars(column_lists[...].reshape(rows, n), 0)
    all_lists[place] = column_lists[...]
    loads[2].wait()
    early.wait()
    lax.fori_loop(1, rows, functools.partial(serve, 0, 0), 0)
    own_wanted = id_scalars[0, 0, row]
    ids_ref[e] = own_wanted
    fetched[e] = table_v[own_wanted]
    row_part = all_lists.at[pl.ds(0, per_row - 1)]
    pltpu.make_async_copy(row_part, row_part, id_sems.at[3]).wait()
    to_scalars(all_lists[...].reshape(n, n), 1).wait()

    quarter = n // 4
    for t in range(max(fwd, 4)):
        if t < 4:
            first = max(rows, t * quarter)
            lax.fori_loop(first, (t + 1) * quarter, functools.partial(serve, 1, t), 0)
        if t < fwd:
            gather_step(t)

    for load in loads[3:]:
        load.wait()
    contract_last = (((1,), (1,)), ((), ()))
    in_logits = jnp.zeros((m, 8, queries), f32)
    for u in range(ring_cuts):
        all_rows = pg[u].reshape(m * 16, cut_width)
        for h in range(2):
            at = (2 * u + h) * cut_width
            part = lax.dot_general(
                all_rows, q_v[:, at : at + cut_width], contract_last, preferred_element_type=f32
            )
            in_logits = in_logits + part.reshape(m, 2, 8, queries)[:, h]
    in_logits = in_logits.reshape(m * 8, queries) * score_scale

    owner_ids = lax.div(neg_ref[...], blocks)
    owner_list = lax.broadcasted_iota(jnp.int32, (n, queries), 0)
    named = jnp.zeros((n, queries), jnp.bool_)
    for k in range(neg_ref.shape[0]):
        named = named | (owner_list == jnp.broadcast_to(owner_ids[k : k + 1, :], (n, queries)))
    usable = jnp.sum(
        jnp.where(owner_row == owner_col, jnp.broadcast_to(counts_ref[...], (n, n)), 0),
        axis=1,
        keepdims=True,
    )
    live = jnp.where(named, jnp.broadcast_to(usable, (n, queries)), 0)
    live = jnp.concatenate([live, live], axis=0) > 0

    def widen(s, carry):
        origin = source(e, s, n)
        at = pl.ds(pl.multiple_of(origin * pieces, pieces), pieces)
        wide[at, :] = fetched[origin].astype(f32)
        return carry

    for t in range(4):
        count = quarter - 1 if t == 0 else quarter
        arrived = fetched.at[pl.ds(0, count)]
        pltpu.make_async_copy(arrived, arrived, f_sems.at[1 + t]).wait()
        lax.fori_loop(t * quarter, (t + 1) * quarter, widen, 0, unroll=4)
    for j in range(groups):
        both = [wide[pl.ds(2 * j + r, n, pieces), :] for r in range(2)]
        hard[:, j * lanes : (j + 1) * lanes] = jnp.concatenate(both, axis=0).astype(bf16)
    hard_logits = (
        lax.dot_general(hard[...], q_v[...], contract_last, preferred_element_type=f32)
        * score_scale
    )

    top = jnp.maximum(
        jnp.max(in_logits, axis=0, keepdims=True),
        jnp.max(jnp.where(live, hard_logits, -jnp.inf), axis=0, keepdims=True),
    )
    total = jnp.sum(jnp.exp(in_logits - top), axis=0, keepdims=True) + jnp.sum(
        jnp.where(live, jnp.exp(hard_logits - top), 0.0), axis=0, keepdims=True
    )
    row_lse = top + jnp.log(total)
    hard_weights = jnp.where(live, jnp.exp(hard_logits - row_lse), 0.0) * score_scale
    hard_w[...] = hard_weights.astype(bf16)
    is_label = lax.broadcasted_iota(jnp.int32, in_logits.shape, 0) == pos_ref[...]
    picked = jnp.sum(jnp.where(is_label, in_logits, 0.0), axis=0, keepdims=True)
    losses_ref[...] = row_lse - picked
    in_weights = (jnp.exp(in_logits - row_lse) - jnp.where(is_label, 1.0, 0.0)) * score_scale
    in_w[...] = in_weights.astype(bf16)

    span = 4 * lanes
    for c in range(width // span):
        part = jnp.dot(
            hard_w[...], q_v[:, c * span : (c + 1) * span], preferred_element_type=f32
        )
        for k in range(4):
            for r in range(2):
                wide[pl.ds(2 * (4 * c + k) + r, n, pieces), :] = part[
                    r * n : (r + 1) * n, k * lanes : (k + 1) * lanes
                ]

    def give(s, carry):
        peer = partner(e, s, n)
        tsend[peer] = wide[pl.ds(pl.multiple_of(peer * pieces, pieces), pieces), :].astype(bf16)
        pltpu.make_async_remote_copy(
            src_ref=tsend.at[peer],
            dst_ref=terms_ref.at[e],
            send_sem=t_sems.at[0],
            recv_sem=t_sems.at[1],
            device_id={"enc": peer},
        ).start()
        return carry

    lax.fori_loop(1, send_group, give, 0)
    tsend[e] = wide[pl.ds(pl.multiple_of(e * pieces, pieces), pieces), :].astype(bf16)
    pltpu.make_async_copy(tsend.at[e], terms_ref.at[e], t_sems.at[1]).start()

    for c in range(width // span):
        part = jnp.dot(
            in_w[...], q_v[:, c * span : (c + 1) * span], preferred_element_type=f32
        )
        u, at = divmod(c * span, 2 * cut_width)
        h, at = divmod(at, cut_width)
        pgp[u, :, 8 * h : 8 * h + 8, at : at + span] = part.reshape(m, 8, span)

    def carry_on(side, u, t):
        return pltpu.make_async_remote_copy(
            src_ref=rs_send.at[side, u, t],
            dst_ref=rs_recv.at[side, u, t],
            send_sem=r_send.at[side, u, t],
            recv_sem=r_recv.at[side, u, t],
            device_id={"pb": down if side else up},
        )

    def reduce_step(t):
        for u in range(ring_cuts):
            for side, steps in ((0, fwd), (1, bwd)):
                if t >= steps:
                    continue
                target = lax.rem(z + m - (steps - t) if side else z + steps - t, m)
                held = pgp[u, target]
                if t > 0:
                    carry_on(side, u, t - 1).wait_recv()
                    held = held + rs_recv[side, u, t - 1].astype(f32)
                rs_send[side, u, t] = held.astype(bf16)
                carry_on(side, u, t).start()

    for t in range(max(fwd, n // send_group)):
        if t < fwd:
            reduce_step(t)
        if t > 0 and t * send_group < n:
            lax.fori_loop(t * send_group, min(n, (t + 1) * send_group), give, 0)
    for u in range(ring_cuts):
        carry_on(0, u, fwd - 1).wait_recv()
        carry_on(1, u, bwd - 1).wait_recv()
        done = (
            pgp[u, z] + rs_recv[0, u, fwd - 1].astype(f32) + rs_recv[1, u, bwd - 1].astype(f32)
        )
        at = 2 * u * cut_width
        pgrad_ref[:, at : at + cut_width] = done[:8]
        pgrad_ref[:, at + cut_width : at + 2 * cut_width] = done[8:]

    pltpu.make_async_copy(column_part, column_part, id_sems.at[0]).wait()
    pltpu.make_async_copy(row_part, row_part, id_sems.at[2]).wait()
    pltpu.make_async_copy(
        fsend.at[pl.ds(0, n - 1)], fsend.at[pl.ds(0, n - 1)], f_sems.at[0]
    ).wait()
    for side in range(2):
        for t in range(bwd if side else fwd):
            for u in range(ring_cuts):
                pass_on(side, u, t).wait_send()
                carry_on(side, u, t).wait_send()
    pltpu.make_async_copy(
        tsend.at[pl.ds(0, n - 1)], tsend.at[pl.ds(0, n - 1)], t_sems.at[0]
    ).wait()
    pltpu.make_async_copy(terms_ref, terms_ref, t_sems.at[1]).wait()


def collect_kernel(
    ids_ref, terms_hbm, losses_ref, pgrad_ref, out_ref, losses_out, pgrad_out, terms_ref, sems
):
    copies = [
        pltpu.make_async_copy(losses_ref, losses_out, sems.at[0]),
        pltpu.make_async_copy(pgrad_ref, pgrad_out, sems.at[1]),
    ]
    group = terms_hbm.shape[0] // collect_groups
    for g in range(collect_groups):
        some = pl.ds(g * group, group)
        copies.append(
            pltpu.make_async_copy(terms_hbm.at[some], terms_ref.at[some], sems.at[2 + g])
        )
    for copy in copies[2:] + copies[:2]:
        copy.start()
    out_ref[...] = jnp.zeros_like(out_ref)

    def add(s, carry):
        out_ref[ids_ref[s]] += terms_ref[s].astype(f32)
        return carry

    for g in range(collect_groups):
        copies[2 + g].wait()
        lax.fori_loop(g * group, (g + 1) * group, add, 0, unroll=4)
    for copy in copies[:2]:
        copy.wait()


def body(queries, passages, table, neg_blocks, block_lists, block_counts, pos_index):
    n = lax.axis_size("enc")
    m = lax.axis_size("pb")
    query_rows = queries[0]
    count, width = query_rows.shape
    blocks = table.shape[1]
    pieces = 2 * width // lanes
    per_row = chips_x * cores
    cut_width = width // (2 * ring_cuts)
    table_rows = (
        table[0]
        .reshape(blocks, 2, width // lanes, lanes)
        .transpose(0, 2, 1, 3)
        .reshape(blocks, pieces, lanes)
    )
    whole = pl.BlockSpec(memory_space=pltpu.VMEM)
    in_hbm = pl.BlockSpec(memory_space=pltpu.HBM)
    anywhere = pl.BlockSpec(memory_space=pl.ANY)
    losses, passage_grads, terms, ids = pl.pallas_call(
        functools.partial(exchange_kernel, n, m),
        out_shape=(
            jax.ShapeDtypeStruct((1, count), f32),
            jax.ShapeDtypeStruct((8, width), f32),
            jax.ShapeDtypeStruct((n, pieces, lanes), bf16),
            jax.ShapeDtypeStruct((n,), jnp.int32),
        ),
        in_specs=[in_hbm] * 7,
        out_specs=(whole, whole, anywhere, pl.BlockSpec(memory_space=pltpu.SMEM)),
        scratch_shapes=[
            pltpu.VMEM((count, width), bf16),
            pltpu.VMEM((8, width), bf16),
            pltpu.VMEM((blocks, pieces, lanes), bf16),
            pltpu.VMEM((neg_blocks.shape[2], count), jnp.int32),
            pltpu.VMEM((1, n), jnp.int32),
            pltpu.VMEM((1, count), jnp.int32),
            pltpu.VMEM((n // per_row, 1, n), jnp.int32),
            pltpu.VMEM((per_row, n // per_row, 1, n), jnp.int32),
            pltpu.VMEM((2, 1, n), jnp.int32),
            pltpu.SMEM((2, 1, n), jnp.int32),
            pltpu.VMEM((n, pieces, lanes), bf16),
            pltpu.VMEM((n, pieces, lanes), bf16),
            pltpu.VMEM((n * pieces, lanes), f32),
            pltpu.VMEM((2 * n, width), bf16),
            pltpu.VMEM((ring_cuts, m, 16, cut_width), bf16),
            pltpu.VMEM((2 * n, count), bf16),
            pltpu.VMEM((8 * m, count), bf16),
            pltpu.VMEM((ring_cuts, m, 16, cut_width), f32),
            pltpu.VMEM((n, pieces, lanes), bf16),
            pltpu.VMEM((2, ring_cuts, m // 2, 16, cut_width), bf16),
            pltpu.VMEM((2, ring_cuts, m // 2, 16, cut_width), bf16),
            pltpu.SemaphoreType.DMA((9,)),
            pltpu.SemaphoreType.DMA((4,)),
            pltpu.SemaphoreType.DMA((5,)),
            pltpu.SemaphoreType.DMA((2,)),
            pltpu.SemaphoreType.DMA((2, ring_cuts, m // 2)),
            pltpu.SemaphoreType.DMA((2, ring_cuts, m // 2)),
            pltpu.SemaphoreType.DMA((2, ring_cuts, m // 2)),
            pltpu.SemaphoreType.DMA((2, ring_cuts, m // 2)),
        ],
        compiler_params=pltpu.CompilerParams(
            collective_id=0, has_side_effects=True, vmem_limit_bytes=60 << 20
        ),
        name="exchange",
    )(
        query_rows,
        passages[0],
        table_rows,
        neg_blocks[0].T,
        block_lists[0, 0].reshape(1, n),
        block_counts[0],
        pos_index,
    )
    table_grads, losses, passage_grads = pl.pallas_call(
        collect_kernel,
        out_shape=(
            jax.ShapeDtypeStruct((blocks, pieces, lanes), f32),
            jax.ShapeDtypeStruct((1, count), f32),
            jax.ShapeDtypeStruct((8, width), f32),
        ),
        in_specs=[
            pl.BlockSpec(memory_space=pltpu.SMEM),
            anywhere,
            anywhere,
            anywhere,
        ],
        out_specs=(whole, whole, whole),
        scratch_shapes=[
            pltpu.VMEM((n, pieces, lanes), bf16),
            pltpu.SemaphoreType.DMA((2 + collect_groups,)),
        ],
        compiler_params=pltpu.CompilerParams(vmem_limit_bytes=60 << 20),
        name="collect",
    )(ids, terms, losses, passage_grads)
    table_grads = (
        table_grads.reshape(blocks, width // lanes, 2, lanes)
        .transpose(0, 2, 1, 3)
        .reshape(1, blocks, 2, width)
    )
    return (losses, passage_grads[None], table_grads)


def solution(mesh):
    in_specs = (
        P("enc", "pb", None),
        P("enc", "pb", None),
        P("pb", "enc", None, None),
        P("enc", "pb", None),
        P("enc", "pb", None, None),
        P("enc", "pb", None),
        P("enc", "pb"),
    )
    out_specs = (P("enc", "pb"), P("enc", "pb", None), P("pb", "enc", None, None))
    return jax.shard_map(body, mesh=mesh, in_specs=in_specs, out_specs=out_specs, check_vma=False)
```

```python
import functools

import jax
import jax.numpy as jnp
from jax import lax
from jax.experimental import pallas as pl
from jax.experimental.pallas import tpu as pltpu
from jax.sharding import PartitionSpec as P

score_scale = 50.0
lanes = 128
chips_x = 4
cores = 2
ring_cuts = 2
send_group = 16
collect_groups = 4
f32 = jnp.float32
bf16 = jnp.bfloat16


def zigzag(k, count):
    odd = k % 2
    return lax.rem(odd * ((k + 1) // 2) + (1 - odd) * (count - k // 2), count)


def partner(me, step, count):
    rows = count // (chips_x * cores)
    y = lax.rem(me // (chips_x * cores) + zigzag(step % rows, rows), rows)
    x = lax.rem((me // cores) % chips_x + zigzag((step // rows) % chips_x, chips_x), chips_x)
    core = lax.rem(me % cores + step // (rows * chips_x), cores)
    return (y * chips_x + x) * cores + core


def source(me, step, count):
    rows = count // (chips_x * cores)
    y = lax.rem(me // (chips_x * cores) + rows - zigzag(step % rows, rows), rows)
    x = lax.rem(
        (me // cores) % chips_x + chips_x - zigzag((step // rows) % chips_x, chips_x), chips_x
    )
    core = lax.rem(me % cores + step // (rows * chips_x), cores)
    return (y * chips_x + x) * cores + core


def exchange_kernel(
    n,
    m,
    q_hbm,
    p_hbm,
    table_hbm,
    neg_hbm,
    lists_hbm,
    counts_hbm,
    pos_hbm,
    losses_ref,
    pgrad_ref,
    terms_ref,
    ids_ref,
    q_v,
    p_ref,
    table_v,
    neg_ref,
    counts_ref,
    pos_ref,
    column_lists,
    all_lists,
    id_row,
    id_scalars,
    fsend,
    fetched,
    wide,
    hard,
    pg,
    hard_w,
    in_w,
    pgp,
    tsend,
    rs_send,
    rs_recv,
    local_sem,
    id_sems,
    f_sems,
    t_sems,
    g_send,
    g_recv,
    r_send,
    r_recv,
):
    e = lax.axis_index("enc")
    z = lax.axis_index("pb")
    fwd = m // 2
    bwd = m - 1 - fwd
    up = lax.rem(z + 1, m)
    down = lax.rem(z + m - 1, m)
    pieces = fetched.shape[1]
    groups = pieces // 2
    pitch = pieces + 8
    width = q_v.shape[1]
    cut_width = pg.shape[3]
    per_row = chips_x * cores
    rows = n // per_row
    row, place = e // per_row, e % per_row
    queries = q_v.shape[0]
    blocks = table_v.shape[0]

    barrier = pltpu.get_barrier_semaphore()

    def row_mate(k):
        return {"enc": row * per_row + lax.rem(place + k, per_row)}

    def column_mate(k):
        return {"enc": lax.rem(row + k, rows) * per_row + place}

    for k in range(1, per_row):
        pl.semaphore_signal(barrier, inc=1, device_id=row_mate(k))
    for k in range(1, rows):
        pl.semaphore_signal(barrier, inc=1, device_id=column_mate(k))
    pl.semaphore_signal(barrier, inc=1, device_id={"pb": up})
    pl.semaphore_signal(barrier, inc=1, device_id={"pb": down})
    loads = [
        pltpu.make_async_copy(source, place, local_sem.at[k])
        for k, (source, place) in enumerate(
            (
                (lists_hbm, column_lists.at[row]),
                (p_hbm, p_ref),
                (table_hbm, table_v),
                (counts_hbm, counts_ref),
                (neg_hbm, neg_ref),
                (pos_hbm, pos_ref),
                (q_hbm, q_v),
            )
        )
    ]
    for load in loads:
        load.start()

    owner_row = lax.broadcasted_iota(jnp.int32, (n, n), 0)
    owner_col = lax.broadcasted_iota(jnp.int32, (n, n), 1)
    loads[1].wait()
    own_rows = p_ref[...].astype(f32)
    for u in range(ring_cuts):
        at = 2 * u * cut_width
        halves = [own_rows[:, at + h * cut_width : at + (h + 1) * cut_width] for h in range(2)]
        pg[u, z] = jnp.concatenate(halves, axis=0).astype(bf16)
    loads[0].wait()

    pl.semaphore_wait(barrier, per_row + rows)

    def ring_copy(side, u, t, origin):
        return pltpu.make_async_remote_copy(
            src_ref=pg.at[u, origin],
            dst_ref=pg.at[u, origin],
            send_sem=g_send.at[side, u, t],
            recv_sem=g_recv.at[side, u, t],
            device_id={"pb": down if side else up},
        )

    def pass_on(side, u, t):
        return ring_copy(side, u, t, lax.rem(z + t if side else z + m - t, m))

    def arrival(side, u, t):
        return ring_copy(side, u, t, lax.rem(z + t + 1 if side else z + m - t - 1, m))

    def gather_step(t):
        for u in range(ring_cuts):
            for side, steps in ((0, fwd), (1, bwd)):
                if t < steps:
                    arrival(side, u, t).wait_recv()
                if t + 1 < steps:
                    pass_on(side, u, t + 1).start()

    def column_copy(k):
        return pltpu.make_async_remote_copy(
            src_ref=column_lists.at[row],
            dst_ref=column_lists.at[row],
            send_sem=id_sems.at[0],
            recv_sem=id_sems.at[1],
            device_id=column_mate(k),
        )

    def row_copy(k):
        return pltpu.make_async_remote_copy(
            src_ref=column_lists,
            dst_ref=all_lists.at[place],
            send_sem=id_sems.at[2],
            recv_sem=id_sems.at[3],
            device_id=row_mate(k),
        )

    def to_scalars(lists, slot):
        wanted = jnp.sum(
            jnp.where(owner_col[: lists.shape[0]] == e, lists, 0), axis=1, keepdims=True
        )
        id_row[slot] = jnp.sum(
            jnp.where(
                owner_row[: lists.shape[0]] == owner_col[: lists.shape[0]],
                jnp.broadcast_to(wanted, lists.shape),
                0,
            ),
            axis=0,
            keepdims=True,
        )
        copy = pltpu.make_async_copy(id_row.at[slot], id_scalars.at[slot], local_sem.at[7 + slot])
        copy.start()
        return copy

    def serve(slot, group, s, carry):
        peer = partner(e, s, n)
        asker = peer // per_row if slot == 0 else (peer % per_row) * rows + peer // per_row
        wanted = id_scalars[slot, 0, asker]
        ids_ref[peer] = wanted
        fsend[peer] = table_v[wanted]
        pltpu.make_async_remote_copy(
            src_ref=fsend.at[peer],
            dst_ref=fetched.at[e],
            send_sem=f_sems.at[0],
            recv_sem=f_sems.at[1 + group],
            device_id={"enc": peer},
        ).start()
        return carry

    for k in range(1, rows):
        column_copy(k).start()
    for u in range(ring_cuts):
        pass_on(0, u, 0).start()
        pass_on(1, u, 0).start()
    column_part = column_lists.at[pl.ds(0, rows - 1)]
    pltpu.make_async_copy(column_part, column_part, id_sems.at[1]).wait()
    for k in range(1, per_row):
        row_copy(k).start()
    early = to_scalars(column_lists[...].reshape(rows, n), 0)
    all_lists[place] = column_lists[...]
    loads[2].wait()
    early.wait()
    lax.fori_loop(1, rows, functools.partial(serve, 0, 0), 0)
    own_wanted = id_scalars[0, 0, row]
    ids_ref[e] = own_wanted
    fetched[e] = table_v[own_wanted]
    row_part = all_lists.at[pl.ds(0, per_row - 1)]
    pltpu.make_async_copy(row_part, row_part, id_sems.at[3]).wait()
    to_scalars(all_lists[...].reshape(n, n), 1).wait()

    quarter = n // 4
    for t in range(max(fwd, 4)):
        if t < 4:
            first = max(rows, t * quarter)
            lax.fori_loop(first, (t + 1) * quarter, functools.partial(serve, 1, t), 0)
        if t < fwd:
            gather_step(t)

    for load in loads[3:]:
        load.wait()
    contract_last = (((1,), (1,)), ((), ()))
    in_logits = jnp.zeros((m, 8, queries), f32)
    for u in range(ring_cuts):
        all_rows = pg[u].reshape(m * 16, cut_width)
        for h in range(2):
            at = (2 * u + h) * cut_width
            part = lax.dot_general(
                all_rows, q_v[:, at : at + cut_width], contract_last, preferred_element_type=f32
            )
            in_logits = in_logits + part.reshape(m, 2, 8, queries)[:, h]
    in_logits = in_logits.reshape(m * 8, queries) * score_scale

    owner_ids = lax.div(neg_ref[...], blocks)
    owner_list = lax.broadcasted_iota(jnp.int32, (n, queries), 0)
    named = jnp.zeros((n, queries), jnp.bool_)
    for k in range(neg_ref.shape[0]):
        named = named | (owner_list == jnp.broadcast_to(owner_ids[k : k + 1, :], (n, queries)))
    usable = jnp.sum(
        jnp.where(owner_row == owner_col, jnp.broadcast_to(counts_ref[...], (n, n)), 0),
        axis=1,
        keepdims=True,
    )
    live = jnp.where(named, jnp.broadcast_to(usable, (n, queries)), 0)
    live = jnp.concatenate([live, live], axis=0) > 0

    def widen(s, carry):
        origin = source(e, s, n)
        at = pl.ds(pl.multiple_of(origin * pitch, 8), pieces)
        wide[at, :] = fetched[origin].astype(f32)
        return carry

    for t in range(4):
        count = quarter - 1 if t == 0 else quarter
        arrived = fetched.at[pl.ds(0, count)]
        pltpu.make_async_copy(arrived, arrived, f_sems.at[1 + t]).wait()
        lax.fori_loop(t * quarter, (t + 1) * quarter, widen, 0, unroll=4)
    for j in range(groups):
        both = [wide[pl.ds(2 * j + r, n, pitch), :] for r in range(2)]
        hard[:, j * lanes : (j + 1) * lanes] = jnp.concatenate(both, axis=0).astype(bf16)
    hard_logits = (
        lax.dot_general(hard[...], q_v[...], contract_last, preferred_element_type=f32)
        * score_scale
    )

    top = jnp.maximum(
        jnp.max(in_logits, axis=0, keepdims=True),
        jnp.max(jnp.where(live, hard_logits, -jnp.inf), axis=0, keepdims=True),
    )
    total = jnp.sum(jnp.exp(in_logits - top), axis=0, keepdims=True) + jnp.sum(
        jnp.where(live, jnp.exp(hard_logits - top), 0.0), axis=0, keepdims=True
    )
    row_lse = top + jnp.log(total)
    hard_weights = jnp.where(live, jnp.exp(hard_logits - row_lse), 0.0) * score_scale
    hard_w[...] = hard_weights.astype(bf16)
    is_label = lax.broadcasted_iota(jnp.int32, in_logits.shape, 0) == pos_ref[...]
    picked = jnp.sum(jnp.where(is_label, in_logits, 0.0), axis=0, keepdims=True)
    losses_ref[...] = row_lse - picked
    in_weights = (jnp.exp(in_logits - row_lse) - jnp.where(is_label, 1.0, 0.0)) * score_scale
    in_w[...] = in_weights.astype(bf16)

    span = 4 * lanes
    for c in range(width // span):
        part = jnp.dot(
            hard_w[...], q_v[:, c * span : (c + 1) * span], preferred_element_type=f32
        )
        for k in range(4):
            for r in range(2):
                wide[pl.ds(2 * (4 * c + k) + r, n, pitch), :] = part[
                    r * n : (r + 1) * n, k * lanes : (k + 1) * lanes
                ]

    def give(s, carry):
        peer = partner(e, s, n)
        tsend[peer] = wide[pl.ds(pl.multiple_of(peer * pitch, 8), pieces), :].astype(bf16)
        pltpu.make_async_remote_copy(
            src_ref=tsend.at[peer],
            dst_ref=terms_ref.at[e],
            send_sem=t_sems.at[0],
            recv_sem=t_sems.at[1],
            device_id={"enc": peer},
        ).start()
        return carry

    for c in range(width // span):
        part = jnp.dot(
            in_w[...], q_v[:, c * span : (c + 1) * span], preferred_element_type=f32
        )
        u, at = divmod(c * span, 2 * cut_width)
        h, at = divmod(at, cut_width)
        pgp[u, :, 8 * h : 8 * h + 8, at : at + span] = part.reshape(m, 8, span)

    def carry_on(side, u, t):
        return pltpu.make_async_remote_copy(
            src_ref=rs_send.at[side, u, t],
            dst_ref=rs_recv.at[side, u, t],
            send_sem=r_send.at[side, u, t],
            recv_sem=r_recv.at[side, u, t],
            device_id={"pb": down if side else up},
        )

    def reduce_step(t):
        for u in range(ring_cuts):
            for side, steps in ((0, fwd), (1, bwd)):
                if t >= steps:
                    continue
                target = lax.rem(z + m - (steps - t) if side else z + steps - t, m)
                held = pgp[u, target]
                if t > 0:
                    carry_on(side, u, t - 1).wait_recv()
                    held = held + rs_recv[side, u, t - 1].astype(f32)
                rs_send[side, u, t] = held.astype(bf16)
                carry_on(side, u, t).start()

    reduce_step(0)
    lax.fori_loop(1, send_group, give, 0)
    tsend[e] = wide[pl.ds(pl.multiple_of(e * pitch, 8), pieces), :].astype(bf16)
    pltpu.make_async_copy(tsend.at[e], terms_ref.at[e], t_sems.at[1]).start()

    for t in range(max(fwd, n // send_group)):
        if 0 < t < fwd:
            reduce_step(t)
        if t > 0 and t * send_group < n:
            lax.fori_loop(t * send_group, min(n, (t + 1) * send_group), give, 0)
    for u in range(ring_cuts):
        carry_on(0, u, fwd - 1).wait_recv()
        carry_on(1, u, bwd - 1).wait_recv()
        done = (
            pgp[u, z] + rs_recv[0, u, fwd - 1].astype(f32) + rs_recv[1, u, bwd - 1].astype(f32)
        )
        at = 2 * u * cut_width
        pgrad_ref[:, at : at + cut_width] = done[:8]
        pgrad_ref[:, at + cut_width : at + 2 * cut_width] = done[8:]

    pltpu.make_async_copy(column_part, column_part, id_sems.at[0]).wait()
    pltpu.make_async_copy(row_part, row_part, id_sems.at[2]).wait()
    pltpu.make_async_copy(
        fsend.at[pl.ds(0, n - 1)], fsend.at[pl.ds(0, n - 1)], f_sems.at[0]
    ).wait()
    for side in range(2):
        for t in range(bwd if side else fwd):
            for u in range(ring_cuts):
                pass_on(side, u, t).wait_send()
                carry_on(side, u, t).wait_send()
    pltpu.make_async_copy(
        tsend.at[pl.ds(0, n - 1)], tsend.at[pl.ds(0, n - 1)], t_sems.at[0]
    ).wait()
    pltpu.make_async_copy(terms_ref, terms_ref, t_sems.at[1]).wait()


def collect_kernel(
    ids_ref, terms_hbm, losses_ref, pgrad_ref, out_ref, losses_out, pgrad_out, terms_ref, sems
):
    copies = [
        pltpu.make_async_copy(losses_ref, losses_out, sems.at[0]),
        pltpu.make_async_copy(pgrad_ref, pgrad_out, sems.at[1]),
    ]
    group = terms_hbm.shape[0] // collect_groups
    for g in range(collect_groups):
        some = pl.ds(g * group, group)
        copies.append(
            pltpu.make_async_copy(terms_hbm.at[some], terms_ref.at[some], sems.at[2 + g])
        )
    for copy in copies[2:] + copies[:2]:
        copy.start()
    out_ref[...] = jnp.zeros_like(out_ref)

    def add(s, carry):
        out_ref[ids_ref[s]] += terms_ref[s].astype(f32)
        return carry

    for g in range(collect_groups):
        copies[2 + g].wait()
        lax.fori_loop(g * group, (g + 1) * group, add, 0, unroll=4)
    for copy in copies[:2]:
        copy.wait()


def body(queries, passages, table, neg_blocks, block_lists, block_counts, pos_index):
    n = lax.axis_size("enc")
    m = lax.axis_size("pb")
    query_rows = queries[0]
    count, width = query_rows.shape
    blocks = table.shape[1]
    pieces = 2 * width // lanes
    per_row = chips_x * cores
    cut_width = width // (2 * ring_cuts)
    table_rows = (
        table[0]
        .reshape(blocks, 2, width // lanes, lanes)
        .transpose(0, 2, 1, 3)
        .reshape(blocks, pieces, lanes)
    )
    whole = pl.BlockSpec(memory_space=pltpu.VMEM)
    in_hbm = pl.BlockSpec(memory_space=pltpu.HBM)
    anywhere = pl.BlockSpec(memory_space=pl.ANY)
    losses, passage_grads, terms, ids = pl.pallas_call(
        functools.partial(exchange_kernel, n, m),
        out_shape=(
            jax.ShapeDtypeStruct((1, count), f32),
            jax.ShapeDtypeStruct((8, width), f32),
            jax.ShapeDtypeStruct((n, pieces, lanes), bf16),
            jax.ShapeDtypeStruct((n,), jnp.int32),
        ),
        in_specs=[in_hbm] * 7,
        out_specs=(whole, whole, anywhere, pl.BlockSpec(memory_space=pltpu.SMEM)),
        scratch_shapes=[
            pltpu.VMEM((count, width), bf16),
            pltpu.VMEM((8, width), bf16),
            pltpu.VMEM((blocks, pieces, lanes), bf16),
            pltpu.VMEM((neg_blocks.shape[2], count), jnp.int32),
            pltpu.VMEM((1, n), jnp.int32),
            pltpu.VMEM((1, count), jnp.int32),
            pltpu.VMEM((n // per_row, 1, n), jnp.int32),
            pltpu.VMEM((per_row, n // per_row, 1, n), jnp.int32),
            pltpu.VMEM((2, 1, n), jnp.int32),
            pltpu.SMEM((2, 1, n), jnp.int32),
            pltpu.VMEM((n, pieces, lanes), bf16),
            pltpu.VMEM((n, pieces, lanes), bf16),
            pltpu.VMEM((n * (pieces + 8), lanes), f32),
            pltpu.VMEM((2 * n, width), bf16),
            pltpu.VMEM((ring_cuts, m, 16, cut_width), bf16),
            pltpu.VMEM((2 * n, count), bf16),
            pltpu.VMEM((8 * m, count), bf16),
            pltpu.VMEM((ring_cuts, m, 16, cut_width), f32),
            pltpu.VMEM((n, pieces, lanes), bf16),
            pltpu.VMEM((2, ring_cuts, m // 2, 16, cut_width), bf16),
            pltpu.VMEM((2, ring_cuts, m // 2, 16, cut_width), bf16),
            pltpu.SemaphoreType.DMA((9,)),
            pltpu.SemaphoreType.DMA((4,)),
            pltpu.SemaphoreType.DMA((5,)),
            pltpu.SemaphoreType.DMA((2,)),
            pltpu.SemaphoreType.DMA((2, ring_cuts, m // 2)),
            pltpu.SemaphoreType.DMA((2, ring_cuts, m // 2)),
            pltpu.SemaphoreType.DMA((2, ring_cuts, m // 2)),
            pltpu.SemaphoreType.DMA((2, ring_cuts, m // 2)),
        ],
        compiler_params=pltpu.CompilerParams(
            collective_id=0, has_side_effects=True, vmem_limit_bytes=60 << 20
        ),
        name="exchange",
    )(
        query_rows,
        passages[0],
        table_rows,
        neg_blocks[0].T,
        block_lists[0, 0].reshape(1, n),
        block_counts[0],
        pos_index,
    )
    table_grads, losses, passage_grads = pl.pallas_call(
        collect_kernel,
        out_shape=(
            jax.ShapeDtypeStruct((blocks, pieces, lanes), f32),
            jax.ShapeDtypeStruct((1, count), f32),
            jax.ShapeDtypeStruct((8, width), f32),
        ),
        in_specs=[
            pl.BlockSpec(memory_space=pltpu.SMEM),
            anywhere,
            anywhere,
            anywhere,
        ],
        out_specs=(whole, whole, whole),
        scratch_shapes=[
            pltpu.VMEM((n, pieces, lanes), bf16),
            pltpu.SemaphoreType.DMA((2 + collect_groups,)),
        ],
        compiler_params=pltpu.CompilerParams(vmem_limit_bytes=60 << 20),
        name="collect",
    )(ids, terms, losses, passage_grads)
    table_grads = (
        table_grads.reshape(blocks, width // lanes, 2, lanes)
        .transpose(0, 2, 1, 3)
        .reshape(1, blocks, 2, width)
    )
    return (losses, passage_grads[None], table_grads)


def solution(mesh):
    in_specs = (
        P("enc", "pb", None),
        P("enc", "pb", None),
        P("pb", "enc", None, None),
        P("enc", "pb", None),
        P("enc", "pb", None, None),
        P("enc", "pb", None),
        P("enc", "pb"),
    )
    out_specs = (P("enc", "pb"), P("enc", "pb", None), P("pb", "enc", None, None))
    return jax.shard_map(body, mesh=mesh, in_specs=in_specs, out_specs=out_specs, check_vma=False)
```

```python
import functools

import jax
import jax.numpy as jnp
from jax import lax
from jax.experimental import pallas as pl
from jax.experimental.pallas import tpu as pltpu
from jax.sharding import PartitionSpec as P

score_scale = 50.0
lanes = 128
chips_x = 4
cores = 2
ring_cuts = 2
send_group = 16
collect_groups = 4
f32 = jnp.float32
bf16 = jnp.bfloat16


def zigzag(k, count):
    odd = k % 2
    return lax.rem(odd * ((k + 1) // 2) + (1 - odd) * (count - k // 2), count)


def partner(me, step, count):
    rows = count // (chips_x * cores)
    y = lax.rem(me // (chips_x * cores) + zigzag(step % rows, rows), rows)
    x = lax.rem((me // cores) % chips_x + zigzag((step // rows) % chips_x, chips_x), chips_x)
    core = lax.rem(me % cores + step // (rows * chips_x), cores)
    return (y * chips_x + x) * cores + core


def source(me, step, count):
    rows = count // (chips_x * cores)
    y = lax.rem(me // (chips_x * cores) + rows - zigzag(step % rows, rows), rows)
    x = lax.rem(
        (me // cores) % chips_x + chips_x - zigzag((step // rows) % chips_x, chips_x), chips_x
    )
    core = lax.rem(me % cores + step // (rows * chips_x), cores)
    return (y * chips_x + x) * cores + core


def exchange_kernel(
    n,
    m,
    q_hbm,
    p_hbm,
    table_hbm,
    neg_hbm,
    lists_hbm,
    counts_hbm,
    pos_hbm,
    losses_ref,
    pgrad_ref,
    terms_ref,
    ids_ref,
    q_v,
    p_ref,
    table_v,
    neg_ref,
    counts_ref,
    pos_ref,
    column_lists,
    all_lists,
    id_row,
    id_scalars,
    fsend,
    fetched,
    wide,
    hard,
    pg,
    hard_w,
    in_w,
    pgp,
    tsend,
    rs_send,
    rs_recv,
    local_sem,
    id_sems,
    f_sems,
    t_sems,
    g_send,
    g_recv,
    r_send,
    r_recv,
):
    e = lax.axis_index("enc")
    z = lax.axis_index("pb")
    fwd = m // 2
    bwd = m - 1 - fwd
    up = lax.rem(z + 1, m)
    down = lax.rem(z + m - 1, m)
    pieces = fetched.shape[1]
    groups = pieces // 2
    pitch = pieces + 8
    width = q_v.shape[1]
    cut_width = pg.shape[3]
    per_row = chips_x * cores
    rows = n // per_row
    row, place = e // per_row, e % per_row
    queries = q_v.shape[0]
    blocks = table_v.shape[0]

    barrier = pltpu.get_barrier_semaphore()

    def row_mate(k):
        return {"enc": row * per_row + lax.rem(place + k, per_row)}

    def column_mate(k):
        return {"enc": lax.rem(row + k, rows) * per_row + place}

    for k in range(1, per_row):
        pl.semaphore_signal(barrier, inc=1, device_id=row_mate(k))
    for k in range(1, rows):
        pl.semaphore_signal(barrier, inc=1, device_id=column_mate(k))
    pl.semaphore_signal(barrier, inc=1, device_id={"pb": up})
    pl.semaphore_signal(barrier, inc=1, device_id={"pb": down})
    loads = [
        pltpu.make_async_copy(source, place, local_sem.at[k])
        for k, (source, place) in enumerate(
            (
                (lists_hbm, column_lists.at[row]),
                (p_hbm, p_ref),
                (table_hbm, table_v),
                (counts_hbm, counts_ref),
                (neg_hbm, neg_ref),
                (pos_hbm, pos_ref),
                (q_hbm, q_v),
            )
        )
    ]
    for load in loads:
        load.start()

    owner_row = lax.broadcasted_iota(jnp.int32, (n, n), 0)
    owner_col = lax.broadcasted_iota(jnp.int32, (n, n), 1)
    loads[1].wait()
    own_rows = p_ref[...].astype(f32)
    for u in range(ring_cuts):
        at = 2 * u * cut_width
        halves = [own_rows[:, at + h * cut_width : at + (h + 1) * cut_width] for h in range(2)]
        pg[u, z] = jnp.concatenate(halves, axis=0).astype(bf16)
    loads[0].wait()

    pl.semaphore_wait(barrier, per_row + rows)

    def ring_copy(side, u, t, origin):
        return pltpu.make_async_remote_copy(
            src_ref=pg.at[u, origin],
            dst_ref=pg.at[u, origin],
            send_sem=g_send.at[side, u, t],
            recv_sem=g_recv.at[side, u, t],
            device_id={"pb": down if side else up},
        )

    def pass_on(side, u, t):
        return ring_copy(side, u, t, lax.rem(z + t if side else z + m - t, m))

    def arrival(side, u, t):
        return ring_copy(side, u, t, lax.rem(z + t + 1 if side else z + m - t - 1, m))

    def gather_step(t):
        for u in range(ring_cuts):
            for side, steps in ((0, fwd), (1, bwd)):
                if t < steps:
                    arrival(side, u, t).wait_recv()
                if t + 1 < steps:
                    pass_on(side, u, t + 1).start()

    def column_copy(k):
        return pltpu.make_async_remote_copy(
            src_ref=column_lists.at[row],
            dst_ref=column_lists.at[row],
            send_sem=id_sems.at[0],
            recv_sem=id_sems.at[1],
            device_id=column_mate(k),
        )

    def row_copy(k):
        return pltpu.make_async_remote_copy(
            src_ref=column_lists,
            dst_ref=all_lists.at[place],
            send_sem=id_sems.at[2],
            recv_sem=id_sems.at[3],
            device_id=row_mate(k),
        )

    def to_scalars(lists, slot):
        wanted = jnp.sum(
            jnp.where(owner_col[: lists.shape[0]] == e, lists, 0), axis=1, keepdims=True
        )
        id_row[slot] = jnp.sum(
            jnp.where(
                owner_row[: lists.shape[0]] == owner_col[: lists.shape[0]],
                jnp.broadcast_to(wanted, lists.shape),
                0,
            ),
            axis=0,
            keepdims=True,
        )
        copy = pltpu.make_async_copy(id_row.at[slot], id_scalars.at[slot], local_sem.at[7 + slot])
        copy.start()
        return copy

    def serve(slot, group, s, carry):
        peer = partner(e, s, n)
        asker = peer // per_row if slot == 0 else (peer % per_row) * rows + peer // per_row
        wanted = id_scalars[slot, 0, asker]
        ids_ref[peer] = wanted
        fsend[peer] = table_v[wanted]
        pltpu.make_async_remote_copy(
            src_ref=fsend.at[peer],
            dst_ref=fetched.at[e],
            send_sem=f_sems.at[0],
            recv_sem=f_sems.at[1 + group],
            device_id={"enc": peer},
        ).start()
        return carry

    for k in range(1, rows):
        column_copy(k).start()
    for u in range(ring_cuts):
        pass_on(0, u, 0).start()
        pass_on(1, u, 0).start()
    column_part = column_lists.at[pl.ds(0, rows - 1)]
    pltpu.make_async_copy(column_part, column_part, id_sems.at[1]).wait()
    for k in range(1, per_row):
        row_copy(k).start()
    early = to_scalars(column_lists[...].reshape(rows, n), 0)
    all_lists[place] = column_lists[...]
    loads[2].wait()
    early.wait()
    lax.fori_loop(1, rows, functools.partial(serve, 0, 0), 0)
    own_wanted = id_scalars[0, 0, row]
    ids_ref[e] = own_wanted
    fetched[e] = table_v[own_wanted]
    gather_step(0)
    row_part = all_lists.at[pl.ds(0, per_row - 1)]
    pltpu.make_async_copy(row_part, row_part, id_sems.at[3]).wait()
    to_scalars(all_lists[...].reshape(n, n), 1).wait()

    quarter = n // 4
    for t in range(max(fwd, 4)):
        if t < 4:
            first = max(rows, t * quarter)
            lax.fori_loop(first, (t + 1) * quarter, functools.partial(serve, 1, t), 0)
        if t + 1 < fwd:
            gather_step(t + 1)

    for load in loads[3:]:
        load.wait()
    contract_last = (((1,), (1,)), ((), ()))
    in_logits = jnp.zeros((m, 8, queries), f32)
    for u in range(ring_cuts):
        all_rows = pg[u].reshape(m * 16, cut_width)
        for h in range(2):
            at = (2 * u + h) * cut_width
            part = lax.dot_general(
                all_rows, q_v[:, at : at + cut_width], contract_last, preferred_element_type=f32
            )
            in_logits = in_logits + part.reshape(m, 2, 8, queries)[:, h]
    in_logits = in_logits.reshape(m * 8, queries) * score_scale

    owner_ids = lax.div(neg_ref[...], blocks)
    owner_list = lax.broadcasted_iota(jnp.int32, (n, queries), 0)
    named = jnp.zeros((n, queries), jnp.bool_)
    for k in range(neg_ref.shape[0]):
        named = named | (owner_list == jnp.broadcast_to(owner_ids[k : k + 1, :], (n, queries)))
    usable = jnp.sum(
        jnp.where(owner_row == owner_col, jnp.broadcast_to(counts_ref[...], (n, n)), 0),
        axis=1,
        keepdims=True,
    )
    live = jnp.where(named, jnp.broadcast_to(usable, (n, queries)), 0)
    live = jnp.concatenate([live, live], axis=0) > 0

    def widen(s, carry):
        origin = source(e, s, n)
        at = pl.ds(pl.multiple_of(origin * pitch, 8), pieces)
        wide[at, :] = fetched[origin].astype(f32)
        return carry

    for t in range(4):
        count = quarter - 1 if t == 0 else quarter
        arrived = fetched.at[pl.ds(0, count)]
        pltpu.make_async_copy(arrived, arrived, f_sems.at[1 + t]).wait()
        lax.fori_loop(t * quarter, (t + 1) * quarter, widen, 0, unroll=4)
    for j in range(groups):
        both = [wide[pl.ds(2 * j + r, n, pitch), :] for r in range(2)]
        hard[:, j * lanes : (j + 1) * lanes] = jnp.concatenate(both, axis=0).astype(bf16)
    hard_logits = (
        lax.dot_general(hard[...], q_v[...], contract_last, preferred_element_type=f32)
        * score_scale
    )

    top = jnp.maximum(
        jnp.max(in_logits, axis=0, keepdims=True),
        jnp.max(jnp.where(live, hard_logits, -jnp.inf), axis=0, keepdims=True),
    )
    total = jnp.sum(jnp.exp(in_logits - top), axis=0, keepdims=True) + jnp.sum(
        jnp.where(live, jnp.exp(hard_logits - top), 0.0), axis=0, keepdims=True
    )
    row_lse = top + jnp.log(total)
    hard_weights = jnp.where(live, jnp.exp(hard_logits - row_lse), 0.0) * score_scale
    hard_w[...] = hard_weights.astype(bf16)
    is_label = lax.broadcasted_iota(jnp.int32, in_logits.shape, 0) == pos_ref[...]
    picked = jnp.sum(jnp.where(is_label, in_logits, 0.0), axis=0, keepdims=True)
    losses_ref[...] = row_lse - picked
    in_weights = (jnp.exp(in_logits - row_lse) - jnp.where(is_label, 1.0, 0.0)) * score_scale
    in_w[...] = in_weights.astype(bf16)

    span = 4 * lanes
    for c in range(width // span):
        part = jnp.dot(
            hard_w[...], q_v[:, c * span : (c + 1) * span], preferred_element_type=f32
        )
        for k in range(4):
            for r in range(2):
                wide[pl.ds(2 * (4 * c + k) + r, n, pitch), :] = part[
                    r * n : (r + 1) * n, k * lanes : (k + 1) * lanes
                ]

    def give(s, carry):
        peer = partner(e, s, n)
        tsend[peer] = wide[pl.ds(pl.multiple_of(peer * pitch, 8), pieces), :].astype(bf16)
        pltpu.make_async_remote_copy(
            src_ref=tsend.at[peer],
            dst_ref=terms_ref.at[e],
            send_sem=t_sems.at[0],
            recv_sem=t_sems.at[1],
            device_id={"enc": peer},
        ).start()
        return carry

    for c in range(width // span):
        part = jnp.dot(
            in_w[...], q_v[:, c * span : (c + 1) * span], preferred_element_type=f32
        )
        u, at = divmod(c * span, 2 * cut_width)
        h, at = divmod(at, cut_width)
        pgp[u, :, 8 * h : 8 * h + 8, at : at + span] = part.reshape(m, 8, span)

    def carry_on(side, u, t):
        return pltpu.make_async_remote_copy(
            src_ref=rs_send.at[side, u, t],
            dst_ref=rs_recv.at[side, u, t],
            send_sem=r_send.at[side, u, t],
            recv_sem=r_recv.at[side, u, t],
            device_id={"pb": down if side else up},
        )

    def reduce_step(t):
        for u in range(ring_cuts):
            for side, steps in ((0, fwd), (1, bwd)):
                if t >= steps:
                    continue
                target = lax.rem(z + m - (steps - t) if side else z + steps - t, m)
                held = pgp[u, target]
                if t > 0:
                    carry_on(side, u, t - 1).wait_recv()
                    held = held + rs_recv[side, u, t - 1].astype(f32)
                rs_send[side, u, t] = held.astype(bf16)
                carry_on(side, u, t).start()

    reduce_step(0)
    lax.fori_loop(1, send_group, give, 0)
    tsend[e] = wide[pl.ds(pl.multiple_of(e * pitch, 8), pieces), :].astype(bf16)
    pltpu.make_async_copy(tsend.at[e], terms_ref.at[e], t_sems.at[1]).start()

    for t in range(max(fwd, n // send_group)):
        if 0 < t < fwd:
            reduce_step(t)
        if t > 0 and t * send_group < n:
            lax.fori_loop(t * send_group, min(n, (t + 1) * send_group), give, 0)
    for u in range(ring_cuts):
        carry_on(0, u, fwd - 1).wait_recv()
        carry_on(1, u, bwd - 1).wait_recv()
        done = (
            pgp[u, z] + rs_recv[0, u, fwd - 1].astype(f32) + rs_recv[1, u, bwd - 1].astype(f32)
        )
        at = 2 * u * cut_width
        pgrad_ref[:, at : at + cut_width] = done[:8]
        pgrad_ref[:, at + cut_width : at + 2 * cut_width] = done[8:]

    pltpu.make_async_copy(column_part, column_part, id_sems.at[0]).wait()
    pltpu.make_async_copy(row_part, row_part, id_sems.at[2]).wait()
    pltpu.make_async_copy(
        fsend.at[pl.ds(0, n - 1)], fsend.at[pl.ds(0, n - 1)], f_sems.at[0]
    ).wait()
    for side in range(2):
        for t in range(bwd if side else fwd):
            for u in range(ring_cuts):
                pass_on(side, u, t).wait_send()
                carry_on(side, u, t).wait_send()
    pltpu.make_async_copy(
        tsend.at[pl.ds(0, n - 1)], tsend.at[pl.ds(0, n - 1)], t_sems.at[0]
    ).wait()
    pltpu.make_async_copy(terms_ref, terms_ref, t_sems.at[1]).wait()


def collect_kernel(
    ids_ref, terms_hbm, losses_ref, pgrad_ref, out_ref, losses_out, pgrad_out, terms_ref, sems
):
    copies = [
        pltpu.make_async_copy(losses_ref, losses_out, sems.at[0]),
        pltpu.make_async_copy(pgrad_ref, pgrad_out, sems.at[1]),
    ]
    group = terms_hbm.shape[0] // collect_groups
    for g in range(collect_groups):
        some = pl.ds(g * group, group)
        copies.append(
            pltpu.make_async_copy(terms_hbm.at[some], terms_ref.at[some], sems.at[2 + g])
        )
    for copy in copies[2:] + copies[:2]:
        copy.start()
    out_ref[...] = jnp.zeros_like(out_ref)

    def add(s, carry):
        out_ref[ids_ref[s]] += terms_ref[s].astype(f32)
        return carry

    for g in range(collect_groups):
        copies[2 + g].wait()
        lax.fori_loop(g * group, (g + 1) * group, add, 0, unroll=4)
    for copy in copies[:2]:
        copy.wait()


def body(queries, passages, table, neg_blocks, block_lists, block_counts, pos_index):
    n = lax.axis_size("enc")
    m = lax.axis_size("pb")
    query_rows = queries[0]
    count, width = query_rows.shape
    blocks = table.shape[1]
    pieces = 2 * width // lanes
    per_row = chips_x * cores
    cut_width = width // (2 * ring_cuts)
    table_rows = (
        table[0]
        .reshape(blocks, 2, width // lanes, lanes)
        .transpose(0, 2, 1, 3)
        .reshape(blocks, pieces, lanes)
    )
    whole = pl.BlockSpec(memory_space=pltpu.VMEM)
    in_hbm = pl.BlockSpec(memory_space=pltpu.HBM)
    anywhere = pl.BlockSpec(memory_space=pl.ANY)
    losses, passage_grads, terms, ids = pl.pallas_call(
        functools.partial(exchange_kernel, n, m),
        out_shape=(
            jax.ShapeDtypeStruct((1, count), f32),
            jax.ShapeDtypeStruct((8, width), f32),
            jax.ShapeDtypeStruct((n, pieces, lanes), bf16),
            jax.ShapeDtypeStruct((n,), jnp.int32),
        ),
        in_specs=[in_hbm] * 7,
        out_specs=(whole, whole, anywhere, pl.BlockSpec(memory_space=pltpu.SMEM)),
        scratch_shapes=[
            pltpu.VMEM((count, width), bf16),
            pltpu.VMEM((8, width), bf16),
            pltpu.VMEM((blocks, pieces, lanes), bf16),
            pltpu.VMEM((neg_blocks.shape[2], count), jnp.int32),
            pltpu.VMEM((1, n), jnp.int32),
            pltpu.VMEM((1, count), jnp.int32),
            pltpu.VMEM((n // per_row, 1, n), jnp.int32),
            pltpu.VMEM((per_row, n // per_row, 1, n), jnp.int32),
            pltpu.VMEM((2, 1, n), jnp.int32),
            pltpu.SMEM((2, 1, n), jnp.int32),
            pltpu.VMEM((n, pieces, lanes), bf16),
            pltpu.VMEM((n, pieces, lanes), bf16),
            pltpu.VMEM((n * (pieces + 8), lanes), f32),
            pltpu.VMEM((2 * n, width), bf16),
            pltpu.VMEM((ring_cuts, m, 16, cut_width), bf16),
            pltpu.VMEM((2 * n, count), bf16),
            pltpu.VMEM((8 * m, count), bf16),
            pltpu.VMEM((ring_cuts, m, 16, cut_width), f32),
            pltpu.VMEM((n, pieces, lanes), bf16),
            pltpu.VMEM((2, ring_cuts, m // 2, 16, cut_width), bf16),
            pltpu.VMEM((2, ring_cuts, m // 2, 16, cut_width), bf16),
            pltpu.SemaphoreType.DMA((9,)),
            pltpu.SemaphoreType.DMA((4,)),
            pltpu.SemaphoreType.DMA((5,)),
            pltpu.SemaphoreType.DMA((2,)),
            pltpu.SemaphoreType.DMA((2, ring_cuts, m // 2)),
            pltpu.SemaphoreType.DMA((2, ring_cuts, m // 2)),
            pltpu.SemaphoreType.DMA((2, ring_cuts, m // 2)),
            pltpu.SemaphoreType.DMA((2, ring_cuts, m // 2)),
        ],
        compiler_params=pltpu.CompilerParams(
            collective_id=0, has_side_effects=True, vmem_limit_bytes=60 << 20
        ),
        name="exchange",
    )(
        query_rows,
        passages[0],
        table_rows,
        neg_blocks[0].T,
        block_lists[0, 0].reshape(1, n),
        block_counts[0],
        pos_index,
    )
    table_grads, losses, passage_grads = pl.pallas_call(
        collect_kernel,
        out_shape=(
            jax.ShapeDtypeStruct((blocks, pieces, lanes), f32),
            jax.ShapeDtypeStruct((1, count), f32),
            jax.ShapeDtypeStruct((8, width), f32),
        ),
        in_specs=[
            pl.BlockSpec(memory_space=pltpu.SMEM),
            anywhere,
            anywhere,
            anywhere,
        ],
        out_specs=(whole, whole, whole),
        scratch_shapes=[
            pltpu.VMEM((n, pieces, lanes), bf16),
            pltpu.SemaphoreType.DMA((2 + collect_groups,)),
        ],
        compiler_params=pltpu.CompilerParams(vmem_limit_bytes=60 << 20),
        name="collect",
    )(ids, terms, losses, passage_grads)
    table_grads = (
        table_grads.reshape(blocks, width // lanes, 2, lanes)
        .transpose(0, 2, 1, 3)
        .reshape(1, blocks, 2, width)
    )
    return (losses, passage_grads[None], table_grads)


def solution(mesh):
    in_specs = (
        P("enc", "pb", None),
        P("enc", "pb", None),
        P("pb", "enc", None, None),
        P("enc", "pb", None),
        P("enc", "pb", None, None),
        P("enc", "pb", None),
        P("enc", "pb"),
    )
    out_specs = (P("enc", "pb"), P("enc", "pb", None), P("pb", "enc", None, None))
    return jax.shard_map(body, mesh=mesh, in_specs=in_specs, out_specs=out_specs, check_vma=False)
```
